768 devices in a mesh: blk: 96 (over z_lo, y, x), sub: 8 (over z_hi, core).
Axes of the slice: x: 4, y: 8, z: 12 (z_hi: 4, z_lo: 3; z = z_hi * 3 + z_lo), core: 2. Of those that a mesh axis runs over, the one named last changes fastest.
Arguments:
- image: bfloat16 [393216, 768], P(('blk', 'sub')), may hold values from -0.21582031 to 0.21582031
- text: bfloat16 [393216, 768], P(('blk', 'sub')), may hold values from -0.21582031 to 0.21582031
- scale: float32 [1], replicated, may hold values from 5 to 20
- shift: float32 [1], replicated, may hold values from -6 to -1
Outputs:
- row_loss: float32 [393216], P(('blk', 'sub'))
- image_grad: float32 [393216, 768], P(('blk', 'sub'))
- text_grad: float32 [393216, 768], P(('blk', 'sub'))
The draws below stay inside these ranges and needn't reach their ends.
All inputs are finite; a program needn't handle non-finite values.
Results may differ from the reference program's by a relative error of at most 0.0036.
Values may be sent and summed in bfloat16 or wider, within the bound.
No kernel may reach another device: no remote copies, remote signals or barrier semaphores. Data moves between devices by JAX's collectives and lax.ppermute only.
A program may use at most 32 MiB of HBM per device.

```python
import math
import jax
import jax.numpy as jnp
from jax import lax

D = 768
ROWS = 512
WINDOW = 3
PAIRS = 393216
N_BLK = 96
N_SUB = 8


def block_levels(own_key, dims, cuts, smallest, largest):
    gain = 1.0
    for position, parts in cuts:
        steps = jax.random.uniform(jax.random.fold_in(jax.random.fold_in(own_key, 6), position), (parts,), jnp.float32, smallest / len(cuts), largest / len(cuts))
        gain = gain * jnp.repeat(jnp.exp(steps), dims[position] // parts).reshape((-1,) + (1,) * (len(dims) - 1 - position))
    return gain


def centred(stream_key, extent, width, bound, cuts=(), kind=jnp.bfloat16):
    drawn = width * jax.random.normal(stream_key, extent, jnp.float32)
    if cuts:
        drawn = drawn * block_levels(stream_key, extent, cuts, -0.22, 0.18)
    return jnp.clip(drawn, -bound, bound).astype(kind)


def setup_inputs(seed: int = 0) -> dict:
    key_of = jax.random.split(jax.random.key(seed), 5)
    image = centred(key_of[0], (PAIRS, D), (D ** -0.5), 0.21582031, ((0, 768),))
    text = centred(key_of[1], (PAIRS, D), (D ** -0.5), 0.21582031, ((0, 768),))
    scale = jnp.clip(jnp.exp(jax.random.uniform(key_of[2], (1,), jnp.float32, math.log(5.0), math.log(20.0))), 5.0, 20.0)
    shift = jnp.clip(jax.random.uniform(key_of[3], (1,), jnp.float32, -6.0, -1.0), -6.0, -1.0)
    return {"image": image, "text": text, "scale": scale, "shift": shift}


EPS = 1e-06

def normalize(values):
    full = values.astype(jnp.float32)
    length = jnp.sqrt(lax.optimization_barrier(jnp.sum(full * full, axis=-1, keepdims=True)) + EPS)
    return (full / length, length)

def unit_back(grad, unit, length):
    return (grad - unit * lax.optimization_barrier(jnp.sum(unit * grad, axis=-1, keepdims=True))) / length

def reference(image, text, scale, shift):
    count = N_BLK * N_SUB
    image_unit, image_norm = normalize(image)
    text_unit, text_norm = normalize(text)
    image_blocks = image_unit.astype(jnp.bfloat16).reshape(count, ROWS, D)
    text_blocks = text_unit.astype(jnp.bfloat16).reshape(count, ROWS, D)
    temper = scale[0]
    offset = shift[0]
    diagonal = jnp.eye(ROWS, dtype=jnp.float32)

    def one_block(index):
        rows_here = image_blocks[index]
        loss = jnp.zeros((ROWS,), jnp.float32)
        grad_here = jnp.zeros((ROWS, D), jnp.float32)
        pieces = []
        for turn in range(WINDOW):
            other = text_blocks[(index - turn) % count]
            logits = temper * jnp.dot(rows_here, other.T, preferred_element_type=jnp.float32) + offset
            sign = 2.0 * diagonal - 1.0 if turn == 0 else -1.0
            loss = loss + lax.optimization_barrier(jnp.sum(jax.nn.softplus(-sign * logits), axis=1))
            coef = (-sign * jax.nn.sigmoid(-sign * logits)).astype(jnp.bfloat16)
            grad_here = grad_here + temper * jnp.dot(coef, other, preferred_element_type=jnp.float32)
            pieces.append(temper * jnp.dot(coef.T, rows_here, preferred_element_type=jnp.float32))
        return (loss / ROWS, grad_here) + tuple(pieces)
    results = lax.map(one_block, jnp.arange(count, dtype=jnp.int32))
    row_loss = results[0].reshape(-1)
    unit_image_grad = results[1].reshape(-1, D)
    gathered = results[2]
    for turn in range(1, WINDOW):
        gathered = gathered + jnp.roll(results[2 + turn], -turn, axis=0)
    unit_text_grad = gathered.reshape(-1, D)
    image_grad = unit_back(unit_image_grad, image_unit, image_norm)
    text_grad = unit_back(unit_text_grad, text_unit, text_norm)
    return (row_loss, image_grad, text_grad)
```

```python
import jax
import jax.numpy as jnp
from jax import lax
from jax.experimental import pallas as pl
from jax.experimental.pallas import tpu as pltpu
from jax.sharding import PartitionSpec as P

EPS = 1e-06
AXES = ("blk", "sub")
TILE = 256
F32 = jnp.float32
BF16 = jnp.bfloat16
VMEM = pl.BlockSpec(memory_space=pltpu.VMEM)
SMEM = pl.BlockSpec(memory_space=pltpu.SMEM)
ANY = pl.BlockSpec(memory_space=pl.ANY)
PARAMS = pltpu.CompilerParams(vmem_limit_bytes=16 * 2**20)


def exchange(array, odd_by, even_by):
    count = lax.axis_size(AXES)
    steps = [(i, odd_by if i % 2 else even_by) for i in range(count)]
    return lax.ppermute(array, AXES, [(i, (i + by) % count) for i, by in steps if by is not None])


def exchange_in_parts(array, parts, odd_by, even_by):
    size = array.shape[0] // parts
    return [
        exchange(lax.slice_in_dim(array, at, at + size), odd_by, even_by)
        for at in range(0, array.shape[0], size)
    ]


def is_odd():
    return lax.rem(lax.axis_index("sub"), 2) == 1


def select(odd, one, other, at):
    return jnp.where(odd, one[at, :].astype(F32), other[at, :].astype(F32))


def inverse_norm(full):
    return lax.rsqrt(jnp.sum(full * full, axis=-1, keepdims=True) + EPS)


def products(own, other, temper, offset):
    return temper * lax.dot_general(
        own, other, (((1,), (1,)), ((), ())), preferred_element_type=F32
    ) + offset


def terms(logits, diagonal=None):
    if diagonal is not None:
        logits = jnp.where(diagonal, -logits, logits)
    power = jnp.exp(logits)
    above = 1.0 + power
    plus = jnp.where(
        power < 0.01, power * (1.0 - power * (0.5 - power * (1.0 / 3.0))), jnp.log(above)
    )
    coef = power / above
    if diagonal is not None:
        coef = jnp.where(diagonal, -coef, coef)
    return coef.astype(BF16), jnp.sum(plus, axis=1, keepdims=True)


def weighted(coef, other):
    return jnp.dot(coef, other, preferred_element_type=F32)


def on_diagonal(start, rows, columns):
    row = lax.broadcasted_iota(jnp.int32, (rows, columns), 0) + start
    return row == lax.broadcasted_iota(jnp.int32, (rows, columns), 1)


def finished(acc, raw, inverse, temper):
    grad = temper * acc
    unit = raw * inverse
    return (grad - unit * jnp.sum(unit * grad, axis=-1, keepdims=True)) * inverse


def put(grad, odd, image_grad, text_grad, sems, number, act):
    at = pl.ds(number * TILE, TILE)

    @pl.when(odd)
    def _():
        act(pltpu.make_async_copy(grad.at[at, :], image_grad.at[at, :], sems.at[number]))

    @pl.when(jnp.logical_not(odd))
    def _():
        act(pltpu.make_async_copy(grad.at[at, :], text_grad.at[at, :], sems.at[number]))


def prepare_kernel(image, text, xlow, ylow, xinv, yinv):
    odd = is_odd()
    for start in range(0, image.shape[0], TILE):
        at = pl.ds(start, TILE)
        for low, inv, full in (
            (xlow, xinv, select(odd, image, text, at)),
            (ylow, yinv, select(odd, text, image, at)),
        ):
            inverse = inverse_norm(full)
            inv[at, :] = inverse
            low[at, :] = (full * inverse).astype(BF16)


def arrived_kernel(text_piece, image_piece, low):
    odd = is_odd()
    for start in range(0, low.shape[0], TILE):
        at = pl.ds(start, TILE)
        full = select(odd, text_piece, image_piece, at)
        low[at, :] = (full * inverse_norm(full)).astype(BF16)


def local_kernel(scale, shift, xlow, ylow, *refs):
    pieces, (xacc, yacc, xloss, yloss, xsend) = refs[:-5], refs[-5:]
    temper, offset = scale[0], shift[0]
    rows = xlow.shape[0]
    for start in range(0, rows, TILE):
        at = pl.ds(start, TILE)
        xsend[at, :] = xlow[at, :]
        diagonal = on_diagonal(start, TILE, rows)
        coef, plus = terms(products(xlow[at, :], ylow[...], temper, offset), diagonal)
        acc = weighted(coef, ylow[...])
        for piece in pieces:
            coef, more = terms(products(xlow[at, :], piece[...], temper, offset))
            plus += more
            acc += weighted(coef, piece[...])
        xloss[at, :] = plus
        xacc[at, :] = acc
        coef, plus = terms(products(ylow[at, :], xlow[...], temper, offset), diagonal)
        yloss[at, :] = plus
        yacc[at, :] = weighted(coef, xlow[...])


def first_kernel(
    scale, shift, image, text, xlow, xinv, xacc, xloss_in, low,
    image_grad, text_grad, xloss, grad, sems,
):
    temper, offset = scale[0], shift[0]
    odd = is_odd()
    count = xlow.shape[0] // TILE
    for number in range(count):
        at = pl.ds(number * TILE, TILE)
        coef, plus = terms(products(xlow[at, :], low[...], temper, offset))
        xloss[at, :] = xloss_in[at, :] + plus
        acc = xacc[at, :] + weighted(coef, low[...])
        grad[at, :] = finished(acc, select(odd, image, text, at), xinv[at, :], temper)
        put(grad, odd, image_grad, text_grad, sems, number, lambda copy: copy.start())
    for number in range(count):
        put(grad, odd, image_grad, text_grad, sems, number, lambda copy: copy.wait())


def second_kernel(scale, shift, ylow, yacc_in, yloss_in, xloss, *refs):
    pieces, (yacc, loss) = refs[:-2], refs[-2:]
    temper, offset = scale[0], shift[0]
    odd = is_odd()
    for start in range(0, ylow.shape[0], TILE):
        at = pl.ds(start, TILE)
        total, acc = yloss_in[at, :], yacc_in[at, :]
        for piece in pieces:
            coef, plus = terms(products(ylow[at, :], piece[...], temper, offset))
            total += plus
            acc += weighted(coef, piece[...])
        loss[at, :] = jnp.where(odd, xloss[at, :], total)
        yacc[at, :] = acc


def last_kernel(
    scale, shift, image, text, ylow, yinv, yacc, loss_in, low, image_in, text_in,
    image_grad, text_grad, loss, grad, sems,
):
    del image_in, text_in
    temper, offset = scale[0], shift[0]
    odd = is_odd()
    rows = ylow.shape[0]
    for number in range(rows // TILE):
        at = pl.ds(number * TILE, TILE)
        coef, plus = terms(products(ylow[at, :], low[...], temper, offset))
        acc = yacc[at, :] + weighted(coef, low[...])
        grad[at, :] = finished(acc, select(odd, text, image, at), yinv[at, :], temper)
        put(grad, jnp.logical_not(odd), image_grad, text_grad, sems, number, lambda copy: copy.start())
        total = loss_in[at, :] + jnp.where(odd, 0.0, plus)
        loss[at] = jnp.sum(total, axis=1) * (1.0 / rows)
    for number in range(rows // TILE):
        put(grad, jnp.logical_not(odd), image_grad, text_grad, sems, number, lambda copy: copy.wait())


def cost():
    return pl.CostEstimate(flops=1, bytes_accessed=1, transcendentals=0)


def body(image, text, scale, shift):
    rows, width = image.shape
    text_piece = exchange(text, 2, None)
    image_piece = exchange(image, None, -2)

    wide = jax.ShapeDtypeStruct((rows, width), F32)
    slim = jax.ShapeDtypeStruct((rows, width), BF16)
    thin = jax.ShapeDtypeStruct((rows, 1), F32)
    grads = [pltpu.VMEM((rows, width), F32), pltpu.SemaphoreType.DMA((rows // TILE,))]

    def call(kernel, name, inputs, outs, **more):
        specs = dict(out_specs=(VMEM,) * len(outs), in_specs=[VMEM] * len(inputs))
        specs.update(more)
        return pl.pallas_call(
            kernel, out_shape=outs, compiler_params=PARAMS, cost_estimate=cost(), name=name, **specs
        )(*inputs)

    numbers = (scale, shift)
    xlow, ylow, xinv, yinv = call(prepare_kernel, "prepare", (image, text), (slim, slim, thin, thin))
    r0 = exchange_in_parts(xlow, 2, -1, 1)
    xacc, yacc, xloss, yloss, xsend = call(
        local_kernel, "local", (*numbers, xlow, ylow, *r0), (wide, wide, thin, thin, slim),
        in_specs=[SMEM] * 2 + [VMEM] * (2 + len(r0)),
    )
    r2 = exchange(xsend, -2, 2)
    (r1,) = call(arrived_kernel, "arrived", (text_piece, image_piece), (slim,))
    r3 = exchange_in_parts(r1, 2, -1, 1)
    image_grad, text_grad, xloss = call(
        first_kernel, "first", (*numbers, image, text, xlow, xinv, xacc, xloss, r1), (wide, wide, thin),
        in_specs=[SMEM] * 2 + [VMEM] * 7, out_specs=(ANY, ANY, VMEM), scratch_shapes=grads,
    )
    yacc, loss = call(
        second_kernel, "second", (*numbers, ylow, yacc, yloss, xloss, *r3), (wide, thin),
        in_specs=[SMEM] * 2 + [VMEM] * (4 + len(r3)),
    )
    image_grad, text_grad, loss = call(
        last_kernel, "last",
        (*numbers, image, text, ylow, yinv, yacc, loss, r2, image_grad, text_grad),
        (wide, wide, jax.ShapeDtypeStruct((rows,), F32)),
        in_specs=[SMEM] * 2 + [VMEM] * 7 + [ANY] * 2, out_specs=(ANY, ANY, VMEM), scratch_shapes=grads,
        input_output_aliases={9: 0, 10: 1},
    )
    return loss, image_grad, text_grad


def solution(mesh):
    in_specs = (P(AXES, None), P(AXES, None), P(), P())
    out_specs = (P(AXES), P(AXES, None), P(AXES, None))
    return jax.shard_map(body, mesh=mesh, in_specs=in_specs, out_specs=out_specs, check_vma=False)
```

```python
import jax
import jax.numpy as jnp
from jax import lax
from jax.experimental import pallas as pl
from jax.experimental.pallas import tpu as pltpu
from jax.sharding import PartitionSpec as P

EPS = 1e-06
AXES = ("blk", "sub")
TILE = 256
F32 = jnp.float32
BF16 = jnp.bfloat16
VMEM = pl.BlockSpec(memory_space=pltpu.VMEM)
ANY = pl.BlockSpec(memory_space=pl.ANY)
PARAMS = pltpu.CompilerParams(vmem_limit_bytes=16 * 2**20)


def exchange(array, odd_by, even_by):
    count = lax.axis_size(AXES)
    steps = [(i, odd_by if i % 2 else even_by) for i in range(count)]
    return lax.ppermute(array, AXES, [(i, (i + by) % count) for i, by in steps if by is not None])


def exchange_in_parts(array, parts, odd_by, even_by):
    size = array.shape[0] // parts
    return [
        exchange(lax.slice_in_dim(array, at, at + size), odd_by, even_by)
        for at in range(0, array.shape[0], size)
    ]


def is_odd():
    return lax.rem(lax.axis_index("sub"), 2) == 1


def select(odd, one, other, at):
    return jnp.where(odd, one[at, :].astype(F32), other[at, :].astype(F32))


def inverse_norm(full):
    return lax.rsqrt(jnp.sum(full * full, axis=-1, keepdims=True) + EPS)


def products(own, other, temper, offset):
    return temper * lax.dot_general(
        own, other, (((1,), (1,)), ((), ())), preferred_element_type=F32
    ) + offset


def terms(logits, diagonal=None):
    if diagonal is not None:
        logits = jnp.where(diagonal, -logits, logits)
    power = jnp.exp(logits)
    above = 1.0 + power
    plus = jnp.where(
        power < 0.01, power * (1.0 - power * (0.5 - power * (1.0 / 3.0))), jnp.log(above)
    )
    coef = power / above
    if diagonal is not None:
        coef = jnp.where(diagonal, -coef, coef)
    return coef.astype(BF16), jnp.sum(plus, axis=1, keepdims=True)


def weighted(coef, other):
    return jnp.dot(coef, other, preferred_element_type=F32)


def on_diagonal(start, rows, columns):
    row = lax.broadcasted_iota(jnp.int32, (rows, columns), 0) + start
    return row == lax.broadcasted_iota(jnp.int32, (rows, columns), 1)


def finished(acc, raw, inverse, temper):
    grad = temper * acc
    unit = raw * inverse
    return (grad - unit * jnp.sum(unit * grad, axis=-1, keepdims=True)) * inverse


def prepare_kernel(image, text, xlow, ylow, xinv, yinv):
    odd = is_odd()
    for start in range(0, image.shape[0], TILE):
        at = pl.ds(start, TILE)
        for low, inv, full in (
            (xlow, xinv, select(odd, image, text, at)),
            (ylow, yinv, select(odd, text, image, at)),
        ):
            inverse = inverse_norm(full)
            inv[at, :] = inverse
            low[at, :] = (full * inverse).astype(BF16)


def arrived_kernel(text_piece, image_piece, low):
    odd = is_odd()
    for start in range(0, low.shape[0], TILE):
        at = pl.ds(start, TILE)
        full = select(odd, text_piece, image_piece, at)
        low[at, :] = (full * inverse_norm(full)).astype(BF16)


def local_kernel(scale, shift, xlow, ylow, *refs):
    pieces, (xacc, yacc, xloss, yloss, xsend) = refs[:-5], refs[-5:]
    temper, offset = scale[...], shift[...]
    rows = xlow.shape[0]
    for start in range(0, rows, TILE):
        at = pl.ds(start, TILE)
        xsend[at, :] = xlow[at, :]
        diagonal = on_diagonal(start, TILE, rows)
        coef, plus = terms(products(xlow[at, :], ylow[...], temper, offset), diagonal)
        acc = weighted(coef, ylow[...])
        for piece in pieces:
            coef, more = terms(products(xlow[at, :], piece[...], temper, offset))
            plus += more
            acc += weighted(coef, piece[...])
        xloss[at, :] = plus
        xacc[at, :] = acc
        coef, plus = terms(products(ylow[at, :], xlow[...], temper, offset), diagonal)
        yloss[at, :] = plus
        yacc[at, :] = weighted(coef, xlow[...])


def first_kernel(scale, shift, image, text, xlow, xinv, xacc, xloss_in, low, grad, xloss):
    temper, offset = scale[...], shift[...]
    odd = is_odd()
    starts = range(0, xlow.shape[0], TILE)
    logits = [products(xlow[pl.ds(start, TILE), :], low[...], temper, offset) for start in starts]
    for start, tile in zip(starts, logits):
        at = pl.ds(start, TILE)
        coef, plus = terms(tile)
        xloss[at, :] = xloss_in[at, :] + plus
        acc = xacc[at, :] + weighted(coef, low[...])
        grad[at, :] = finished(acc, select(odd, image, text, at), xinv[at, :], temper)


def second_kernel(scale, shift, ylow, yacc_in, yloss_in, xloss, xgrad, *refs):
    pieces, (yacc, loss, image_grad, text_grad, sem) = refs[:-5], refs[-5:]
    temper, offset = scale[...], shift[...]
    odd = is_odd()

    def run(target):
        copy = pltpu.make_async_copy(xgrad, target, sem)
        copy.start()
        starts = range(0, ylow.shape[0], TILE)
        logits = [
            [products(ylow[pl.ds(start, TILE), :], piece[...], temper, offset) for piece in pieces]
            for start in starts
        ]
        for start, tiles in zip(starts, logits):
            at = pl.ds(start, TILE)
            total, acc = yloss_in[at, :], yacc_in[at, :]
            for piece, tile in zip(pieces, tiles):
                coef, plus = terms(tile)
                total += plus
                acc += weighted(coef, piece[...])
            loss[at, :] = jnp.where(odd, xloss[at, :], total)
            yacc[at, :] = acc
        copy.wait()

    @pl.when(odd)
    def _():
        run(image_grad)

    @pl.when(jnp.logical_not(odd))
    def _():
        run(text_grad)


def last_kernel(
    scale, shift, image, text, ylow, yinv, yacc, loss_in, low, image_in, text_in,
    image_grad, text_grad, loss, ygrad, sems,
):
    del image_in, text_in
    temper, offset = scale[...], shift[...]
    odd = is_odd()

    def run(raw, target, counted):
        rows = ylow.shape[0]
        starts = range(0, rows, TILE)
        copies = [
            pltpu.make_async_copy(
                ygrad.at[pl.ds(start, TILE), :], target.at[pl.ds(start, TILE), :], sems.at[start // TILE]
            )
            for start in starts
        ]
        logits = [products(ylow[pl.ds(start, TILE), :], low[...], temper, offset) for start in starts]
        for start, tile, copy in zip(starts, logits, copies):
            at = pl.ds(start, TILE)
            coef, plus = terms(tile)
            acc = yacc[at, :] + weighted(coef, low[...])
            ygrad[at, :] = finished(acc, raw[at, :].astype(F32), yinv[at, :], temper)
            copy.start()
            total = loss_in[at, :] + plus if counted else loss_in[at, :]
            loss[at] = jnp.sum(total, axis=1) * (1.0 / rows)
        for copy in copies:
            copy.wait()

    @pl.when(odd)
    def _():
        run(text, text_grad, False)

    @pl.when(jnp.logical_not(odd))
    def _():
        run(image, image_grad, True)


def cost():
    return pl.CostEstimate(flops=1, bytes_accessed=1, transcendentals=0)


def body(image, text, scale, shift):
    rows, width = image.shape
    text_piece = exchange(text, 2, None)
    image_piece = exchange(image, None, -2)

    wide = jax.ShapeDtypeStruct((rows, width), F32)
    slim = jax.ShapeDtypeStruct((rows, width), BF16)
    thin = jax.ShapeDtypeStruct((rows, 1), F32)

    def call(kernel, name, inputs, outs, **more):
        specs = dict(out_specs=(VMEM,) * len(outs), in_specs=[VMEM] * len(inputs))
        specs.update(more)
        return pl.pallas_call(
            kernel, out_shape=outs, compiler_params=PARAMS, cost_estimate=cost(), name=name, **specs
        )(*inputs)

    numbers = (scale.reshape(1, 1), shift.reshape(1, 1))
    xlow, ylow, xinv, yinv = call(prepare_kernel, "prepare", (image, text), (slim, slim, thin, thin))
    r0 = exchange_in_parts(xlow, 2, -1, 1)
    xacc, yacc, xloss, yloss, xsend = call(
        local_kernel, "local", (*numbers, xlow, ylow, *r0), (wide, wide, thin, thin, slim),
    )
    r2 = exchange(xsend, -2, 2)
    (r1,) = call(arrived_kernel, "arrived", (text_piece, image_piece), (slim,))
    r3 = exchange_in_parts(r1, 2, -1, 1)
    xgrad, xloss = call(
        first_kernel, "first", (*numbers, image, text, xlow, xinv, xacc, xloss, r1), (wide, thin)
    )
    yacc, loss, image_grad, text_grad = call(
        second_kernel, "second", (*numbers, ylow, yacc, yloss, xloss, xgrad, *r3), (wide, thin, wide, wide),
        out_specs=(VMEM, VMEM, ANY, ANY), scratch_shapes=[pltpu.SemaphoreType.DMA],
    )
    image_grad, text_grad, loss = call(
        last_kernel, "last",
        (*numbers, image, text, ylow, yinv, yacc, loss, r2, image_grad, text_grad),
        (wide, wide, jax.ShapeDtypeStruct((rows,), F32)),
        in_specs=[VMEM] * 9 + [ANY] * 2, out_specs=(ANY, ANY, VMEM), input_output_aliases={9: 0, 10: 1},
        scratch_shapes=[pltpu.VMEM((rows, width), F32), pltpu.SemaphoreType.DMA((rows // TILE,))],
    )
    return loss, image_grad, text_grad


def solution(mesh):
    in_specs = (P(AXES, None), P(AXES, None), P(), P())
    out_specs = (P(AXES), P(AXES, None), P(AXES, None))
    return jax.shard_map(body, mesh=mesh, in_specs=in_specs, out_specs=out_specs, check_vma=False)
```

```python
import jax
import jax.numpy as jnp
from jax import lax
from jax.experimental import pallas as pl
from jax.experimental.pallas import tpu as pltpu
from jax.sharding import PartitionSpec as P

EPS = 1e-06
AXES = ("blk", "sub")
TILE = 256
F32 = jnp.float32
BF16 = jnp.bfloat16
VMEM = pl.BlockSpec(memory_space=pltpu.VMEM)
ANY = pl.BlockSpec(memory_space=pl.ANY)
PARAMS = pltpu.CompilerParams(vmem_limit_bytes=16 * 2**20)


def exchange(array, odd_by, even_by, among=None):
    count = lax.axis_size(AXES)
    steps = [(i, odd_by if i % 2 else even_by) for i in range(count) if among is None or among(i)]
    return lax.ppermute(array, AXES, [(i, (i + by) % count) for i, by in steps if by is not None])


def crosses(index):
    run = lax.axis_size("sub")
    return index % run == 1 or index % run == run - 2


def exchange_in_parts(array, parts, odd_by, even_by):
    size = array.shape[0] // parts
    return [
        exchange(lax.slice_in_dim(array, at, at + size), odd_by, even_by)
        for at in range(0, array.shape[0], size)
    ]


def is_odd():
    return lax.rem(lax.axis_index("sub"), 2) == 1


def select(odd, one, other, at):
    return jnp.where(odd, one[at, :].astype(F32), other[at, :].astype(F32))


def inverse_norm(full):
    return lax.rsqrt(jnp.sum(full * full, axis=-1, keepdims=True) + EPS)


def products(own, other, temper, offset):
    return temper * lax.dot_general(
        own, other, (((1,), (1,)), ((), ())), preferred_element_type=F32
    ) + offset


def terms(logits, diagonal=None):
    if diagonal is not None:
        logits = jnp.where(diagonal, -logits, logits)
    power = jnp.exp(logits)
    above = 1.0 + power
    plus = jnp.where(
        power < 0.01, power * (1.0 - power * (0.5 - power * (1.0 / 3.0))), jnp.log(above)
    )
    coef = power / above
    if diagonal is not None:
        coef = jnp.where(diagonal, -coef, coef)
    return coef.astype(BF16), jnp.sum(plus, axis=1, keepdims=True)


def weighted(coef, other):
    return jnp.dot(coef, other, preferred_element_type=F32)


def on_diagonal(start, rows, columns):
    row = lax.broadcasted_iota(jnp.int32, (rows, columns), 0) + start
    return row == lax.broadcasted_iota(jnp.int32, (rows, columns), 1)


def finished(acc, raw, inverse, temper):
    grad = temper * acc
    unit = raw * inverse
    return (grad - unit * jnp.sum(unit * grad, axis=-1, keepdims=True)) * inverse


def prepare_kernel(image, text, xlow, ylow, xinv, yinv):
    odd = is_odd()
    for start in range(0, image.shape[0], TILE):
        at = pl.ds(start, TILE)
        for low, inv, full in (
            (xlow, xinv, select(odd, image, text, at)),
            (ylow, yinv, select(odd, text, image, at)),
        ):
            inverse = inverse_norm(full)
            inv[at, :] = inverse
            low[at, :] = (full * inverse).astype(BF16)


def arrived_kernel(text_piece, image_piece, after, low):
    del after
    odd = is_odd()
    for start in range(0, low.shape[0], TILE):
        at = pl.ds(start, TILE)
        full = select(odd, text_piece, image_piece, at)
        low[at, :] = (full * inverse_norm(full)).astype(BF16)


def local_kernel(scale, shift, xlow, ylow, acc, loss, xsend):
    temper, offset = scale[...], shift[...]
    rows = xlow.shape[0]
    xsend[...] = xlow[...]
    for start in range(0, rows, TILE):
        at = pl.ds(start, TILE)
        diagonal = on_diagonal(start, TILE, rows)
        coef, plus = terms(products(xlow[at, :], ylow[...], temper, offset), diagonal)
        loss[at, :] = plus
        acc[at, :] = weighted(coef, ylow[...])


def near_kernel(scale, shift, xlow, ylow, acc, loss, *refs):
    pieces, (xacc, yacc, xloss, yloss, xsend) = refs[:-5], refs[-5:]
    temper, offset = scale[...], shift[...]
    rows = xlow.shape[0]
    xsend[...] = xlow[...]
    for start in range(0, rows, TILE):
        at = pl.ds(start, TILE)
        coef, plus = terms(
            products(ylow[at, :], xlow[...], temper, offset), on_diagonal(start, TILE, rows)
        )
        yloss[at, :] = plus
        yacc[at, :] = weighted(coef, xlow[...])
        total, wide = loss[at, :], acc[at, :]
        for piece in pieces:
            coef, plus = terms(products(xlow[at, :], piece[...], temper, offset))
            total += plus
            wide += weighted(coef, piece[...])
        xloss[at, :] = total
        xacc[at, :] = wide


def first_kernel(scale, shift, image, text, xlow, xinv, xacc, xloss_in, low, grad, xloss):
    temper, offset = scale[...], shift[...]
    odd = is_odd()
    starts = range(0, xlow.shape[0], TILE)
    logits = [products(xlow[pl.ds(start, TILE), :], low[...], temper, offset) for start in starts]
    for start, tile in zip(starts, logits):
        at = pl.ds(start, TILE)
        coef, plus = terms(tile)
        xloss[at, :] = xloss_in[at, :] + plus
        acc = xacc[at, :] + weighted(coef, low[...])
        grad[at, :] = finished(acc, select(odd, image, text, at), xinv[at, :], temper)


def second_kernel(scale, shift, ylow, yacc_in, yloss_in, xloss, xgrad, *refs):
    pieces, (yacc, loss, image_grad, text_grad, sem) = refs[:-5], refs[-5:]
    temper, offset = scale[...], shift[...]
    odd = is_odd()

    def run(target):
        copy = pltpu.make_async_copy(xgrad, target, sem)
        copy.start()
        starts = range(0, ylow.shape[0], TILE)
        logits = [
            [products(ylow[pl.ds(start, TILE), :], piece[...], temper, offset) for piece in pieces]
            for start in starts
        ]
        for start, tiles in zip(starts, logits):
            at = pl.ds(start, TILE)
            total, acc = yloss_in[at, :], yacc_in[at, :]
            for piece, tile in zip(pieces, tiles):
                coef, plus = terms(tile)
                total += plus
                acc += weighted(coef, piece[...])
            loss[at, :] = jnp.where(odd, xloss[at, :], total)
            yacc[at, :] = acc
        copy.wait()

    @pl.when(odd)
    def _():
        run(image_grad)

    @pl.when(jnp.logical_not(odd))
    def _():
        run(text_grad)


def last_kernel(
    scale, shift, image, text, ylow, yinv, yacc, loss_in, r2_across, r2, image_in, text_in,
    image_grad, text_grad, loss, ygrad, sems, low,
):
    del image_in, text_in
    temper, offset = scale[...], shift[...]
    odd = is_odd()

    place = lax.axis_index("sub")
    across = jnp.logical_or(place == 0, place == lax.axis_size("sub") - 1)
    low[...] = jnp.where(across, r2_across[...], r2[...])

    def run(raw, target, counted):
        rows = ylow.shape[0]
        starts = range(0, rows, TILE)
        copies = [
            pltpu.make_async_copy(
                ygrad.at[pl.ds(start, TILE), :], target.at[pl.ds(start, TILE), :], sems.at[start // TILE]
            )
            for start in starts
        ]
        logits = [products(ylow[pl.ds(start, TILE), :], low[...], temper, offset) for start in starts]
        for start, tile, copy in zip(starts, logits, copies):
            at = pl.ds(start, TILE)
            coef, plus = terms(tile)
            acc = yacc[at, :] + weighted(coef, low[...])
            ygrad[at, :] = finished(acc, raw[at, :].astype(F32), yinv[at, :], temper)
            copy.start()
            total = loss_in[at, :] + plus if counted else loss_in[at, :]
            loss[at] = jnp.sum(total, axis=1) * (1.0 / rows)
        for copy in copies:
            copy.wait()

    @pl.when(odd)
    def _():
        run(text, text_grad, False)

    @pl.when(jnp.logical_not(odd))
    def _():
        run(image, image_grad, True)


def cost():
    return pl.CostEstimate(flops=1, bytes_accessed=1, transcendentals=0)


def body(image, text, scale, shift):
    rows, width = image.shape
    text_piece = exchange(text, 2, None)
    image_piece = exchange(image, None, -2)

    wide = jax.ShapeDtypeStruct((rows, width), F32)
    slim = jax.ShapeDtypeStruct((rows, width), BF16)
    thin = jax.ShapeDtypeStruct((rows, 1), F32)

    def call(kernel, name, inputs, outs, **more):
        specs = dict(out_specs=(VMEM,) * len(outs), in_specs=[VMEM] * len(inputs))
        specs.update(more)
        return pl.pallas_call(
            kernel, out_shape=outs, compiler_params=PARAMS, cost_estimate=cost(), name=name, **specs
        )(*inputs)

    numbers = (scale.reshape(1, 1), shift.reshape(1, 1))
    xlow, ylow, xinv, yinv = call(prepare_kernel, "prepare", (image, text), (slim, slim, thin, thin))
    r0 = exchange_in_parts(xlow, 2, -1, 1)
    xacc, xloss, xsend = call(local_kernel, "local", (*numbers, xlow, ylow), (wide, thin, slim))
    r2_across = exchange(xsend, -2, 2, crosses)
    xacc, yacc, xloss, yloss, xsend = call(
        near_kernel, "near", (*numbers, xlow, ylow, xacc, xloss, *r0), (wide, wide, thin, thin, slim)
    )
    r2 = exchange(xsend, -2, 2, lambda i: not crosses(i))
    (r1,) = call(
        arrived_kernel, "arrived", (text_piece, image_piece, xloss), (slim,), in_specs=[VMEM, VMEM, ANY]
    )
    r3 = exchange_in_parts(r1, 2, -1, 1)
    xgrad, xloss = call(
        first_kernel, "first", (*numbers, image, text, xlow, xinv, xacc, xloss, r1), (wide, thin)
    )
    yacc, loss, image_grad, text_grad = call(
        second_kernel, "second", (*numbers, ylow, yacc, yloss, xloss, xgrad, *r3), (wide, thin, wide, wide),
        out_specs=(VMEM, VMEM, ANY, ANY), scratch_shapes=[pltpu.SemaphoreType.DMA],
    )
    image_grad, text_grad, loss = call(
        last_kernel, "last",
        (*numbers, image, text, ylow, yinv, yacc, loss, r2_across, r2, image_grad, text_grad),
        (wide, wide, jax.ShapeDtypeStruct((rows,), F32)),
        in_specs=[VMEM] * 10 + [ANY] * 2, out_specs=(ANY, ANY, VMEM), input_output_aliases={10: 0, 11: 1},
        scratch_shapes=[
            pltpu.VMEM((rows, width), F32), pltpu.SemaphoreType.DMA((rows // TILE,)), pltpu.VMEM((rows, width), BF16),
        ],
    )
    return loss, image_grad, text_grad


def solution(mesh):
    in_specs = (P(AXES, None), P(AXES, None), P(), P())
    out_specs = (P(AXES), P(AXES, None), P(AXES, None))
    return jax.shard_map(body, mesh=mesh, in_specs=in_specs, out_specs=out_specs, check_vma=False)
```

```python
import jax
import jax.numpy as jnp
from jax import lax
from jax.experimental import pallas as pl
from jax.experimental.pallas import tpu as pltpu
from jax.sharding import PartitionSpec as P

EPS = 1e-06
AXES = ("blk", "sub")
TILE = 256
F32 = jnp.float32
BF16 = jnp.bfloat16
VMEM = pl.BlockSpec(memory_space=pltpu.VMEM)
ANY = pl.BlockSpec(memory_space=pl.ANY)
PARAMS = pltpu.CompilerParams(vmem_limit_bytes=16 * 2**20)


def exchange(array, odd_by, even_by, among=None):
    count = lax.axis_size(AXES)
    steps = [(i, odd_by if i % 2 else even_by) for i in range(count) if among is None or among(i)]
    return lax.ppermute(array, AXES, [(i, (i + by) % count) for i, by in steps if by is not None])


def crosses(index):
    run = lax.axis_size("sub")
    return index % run == 1 or index % run == run - 2


def exchange_in_parts(array, parts, odd_by, even_by):
    size = array.shape[0] // parts
    return [
        exchange(lax.slice_in_dim(array, at, at + size), odd_by, even_by)
        for at in range(0, array.shape[0], size)
    ]


def is_odd():
    return lax.rem(lax.axis_index("sub"), 2) == 1


def select(odd, one, other, at):
    return jnp.where(odd, one[at, :].astype(F32), other[at, :].astype(F32))


def inverse_norm(full):
    return lax.rsqrt(jnp.sum(full * full, axis=-1, keepdims=True) + EPS)


def products(own, other, temper, offset):
    return temper * lax.dot_general(
        own, other, (((1,), (1,)), ((), ())), preferred_element_type=F32
    ) + offset


def terms(logits, diagonal=None):
    if diagonal is not None:
        logits = jnp.where(diagonal, -logits, logits)
    power = jnp.exp(logits)
    above = 1.0 + power
    plus = jnp.where(
        power < 0.01, power * (1.0 - power * (0.5 - power * (1.0 / 3.0))), jnp.log(above)
    )
    coef = power / above
    if diagonal is not None:
        coef = jnp.where(diagonal, -coef, coef)
    return coef.astype(BF16), jnp.sum(plus, axis=1, keepdims=True)


def weighted(coef, other):
    return jnp.dot(coef, other, preferred_element_type=F32)


def on_diagonal(start, rows, columns):
    row = lax.broadcasted_iota(jnp.int32, (rows, columns), 0) + start
    return row == lax.broadcasted_iota(jnp.int32, (rows, columns), 1)


def finished(acc, raw, inverse, temper):
    grad = temper * acc
    unit = raw * inverse
    return (grad - unit * jnp.sum(unit * grad, axis=-1, keepdims=True)) * inverse


def prepare_kernel(image, text, xlow, ylow, xinv, yinv):
    odd = is_odd()
    for start in range(0, image.shape[0], TILE):
        at = pl.ds(start, TILE)
        for low, inv, full in (
            (xlow, xinv, select(odd, image, text, at)),
            (ylow, yinv, select(odd, text, image, at)),
        ):
            inverse = inverse_norm(full)
            inv[at, :] = inverse
            low[at, :] = (full * inverse).astype(BF16)


def arrived_kernel(text_piece, image_piece, after, low):
    del after
    odd = is_odd()
    for start in range(0, low.shape[0], TILE):
        at = pl.ds(start, TILE)
        full = select(odd, text_piece, image_piece, at)
        low[at, :] = (full * inverse_norm(full)).astype(BF16)


def local_kernel(scale, shift, xlow, ylow, acc, loss, xsend):
    temper, offset = scale[...], shift[...]
    rows = xlow.shape[0]
    xsend[...] = xlow[...]
    for start in range(0, rows, TILE):
        at = pl.ds(start, TILE)
        diagonal = on_diagonal(start, TILE, rows)
        coef, plus = terms(products(xlow[at, :], ylow[...], temper, offset), diagonal)
        loss[at, :] = plus
        acc[at, :] = weighted(coef, ylow[...])


def near_kernel(scale, shift, xlow, ylow, acc, loss, *refs):
    pieces, (xacc, yacc, xloss, yloss, xsend) = refs[:-5], refs[-5:]
    temper, offset = scale[...], shift[...]
    rows = xlow.shape[0]
    xsend[...] = xlow[...]
    for start in range(0, rows, TILE):
        at = pl.ds(start, TILE)
        coef, plus = terms(
            products(ylow[at, :], xlow[...], temper, offset), on_diagonal(start, TILE, rows)
        )
        yloss[at, :] = plus
        yacc[at, :] = weighted(coef, xlow[...])
        total, wide = loss[at, :], acc[at, :]
        for piece in pieces:
            coef, plus = terms(products(xlow[at, :], piece[...], temper, offset))
            total += plus
            wide += weighted(coef, piece[...])
        xloss[at, :] = total
        xacc[at, :] = wide


def first_kernel(scale, shift, image, text, xlow, xinv, xacc, xloss_in, low, grad, xloss):
    temper, offset = scale[...], shift[...]
    odd = is_odd()
    starts = range(0, xlow.shape[0], TILE)
    logits = [products(xlow[pl.ds(start, TILE), :], low[...], temper, offset) for start in starts]
    for start, tile in zip(starts, logits):
        at = pl.ds(start, TILE)
        coef, plus = terms(tile)
        xloss[at, :] = xloss_in[at, :] + plus
        acc = xacc[at, :] + weighted(coef, low[...])
        grad[at, :] = finished(acc, select(odd, image, text, at), xinv[at, :], temper)


def second_kernel(scale, shift, ylow, yacc_in, yloss_in, xloss, xgrad, *refs):
    pieces, (yacc, loss, mean, image_grad, text_grad, sem) = refs[:-6], refs[-6:]
    temper, offset = scale[...], shift[...]
    odd = is_odd()

    def run(target):
        copy = pltpu.make_async_copy(xgrad, target, sem)
        copy.start()
        starts = range(0, ylow.shape[0], TILE)
        logits = [
            [products(ylow[pl.ds(start, TILE), :], piece[...], temper, offset) for piece in pieces]
            for start in starts
        ]
        for start, tiles in zip(starts, logits):
            at = pl.ds(start, TILE)
            total, acc = yloss_in[at, :], yacc_in[at, :]
            for piece, tile in zip(pieces, tiles):
                coef, plus = terms(tile)
                total += plus
                acc += weighted(coef, piece[...])
            loss[at, :] = total
            mean[at] = jnp.sum(xloss[at, :], axis=1) * (1.0 / ylow.shape[0])
            yacc[at, :] = acc
        copy.wait()

    @pl.when(odd)
    def _():
        run(image_grad)

    @pl.when(jnp.logical_not(odd))
    def _():
        run(text_grad)


def last_kernel(
    scale, shift, image, text, ylow, yinv, yacc, loss_in, mean, r2_across, r2, image_in, text_in,
    image_grad, text_grad, loss, ygrad, sems, low,
):
    del image_in, text_in
    temper, offset = scale[...], shift[...]
    odd = is_odd()

    place = lax.axis_index("sub")
    across = jnp.logical_or(place == 0, place == lax.axis_size("sub") - 1)
    low[...] = jnp.where(across, r2_across[...], r2[...])

    def run(raw, target, counted):
        rows = ylow.shape[0]
        starts = range(0, rows, TILE)
        copies = [
            pltpu.make_async_copy(
                ygrad.at[pl.ds(start, TILE), :], target.at[pl.ds(start, TILE), :], sems.at[start // TILE]
            )
            for start in starts
        ]
        logits = [products(ylow[pl.ds(start, TILE), :], low[...], temper, offset) for start in starts]
        for start, tile, copy in zip(starts, logits, copies):
            at = pl.ds(start, TILE)
            coef, plus = terms(tile)
            acc = yacc[at, :] + weighted(coef, low[...])
            ygrad[at, :] = finished(acc, raw[at, :].astype(F32), yinv[at, :], temper)
            copy.start()
            if counted:
                loss[at] = jnp.sum(loss_in[at, :] + plus, axis=1) * (1.0 / rows)
            else:
                loss[at] = mean[at]
        for copy in copies:
            copy.wait()

    @pl.when(odd)
    def _():
        run(text, text_grad, False)

    @pl.when(jnp.logical_not(odd))
    def _():
        run(image, image_grad, True)


def cost():
    return pl.CostEstimate(flops=1, bytes_accessed=1, transcendentals=0)


def body(image, text, scale, shift):
    rows, width = image.shape
    text_piece = exchange(text, 2, None)
    image_piece = exchange(image, None, -2)

    wide = jax.ShapeDtypeStruct((rows, width), F32)
    slim = jax.ShapeDtypeStruct((rows, width), BF16)
    thin = jax.ShapeDtypeStruct((rows, 1), F32)
    flat = jax.ShapeDtypeStruct((rows,), F32)

    def call(kernel, name, inputs, outs, **more):
        specs = dict(out_specs=(VMEM,) * len(outs), in_specs=[VMEM] * len(inputs))
        specs.update(more)
        return pl.pallas_call(
            kernel, out_shape=outs, compiler_params=PARAMS, cost_estimate=cost(), name=name, **specs
        )(*inputs)

    numbers = (scale.reshape(1, 1), shift.reshape(1, 1))
    xlow, ylow, xinv, yinv = call(prepare_kernel, "prepare", (image, text), (slim, slim, thin, thin))
    r0 = exchange_in_parts(xlow, 2, -1, 1)
    xacc, xloss, xsend = call(local_kernel, "local", (*numbers, xlow, ylow), (wide, thin, slim))
    r2_across = exchange(xsend, -2, 2, crosses)
    xacc, yacc, xloss, yloss, xsend = call(
        near_kernel, "near", (*numbers, xlow, ylow, xacc, xloss, *r0), (wide, wide, thin, thin, slim)
    )
    r2 = exchange(xsend, -2, 2, lambda i: not crosses(i))
    (r1,) = call(
        arrived_kernel, "arrived", (text_piece, image_piece, xloss), (slim,), in_specs=[VMEM, VMEM, ANY]
    )
    r3 = exchange_in_parts(r1, 2, -1, 1)
    xgrad, xloss = call(
        first_kernel, "first", (*numbers, image, text, xlow, xinv, xacc, xloss, r1), (wide, thin)
    )
    yacc, loss, mean, image_grad, text_grad = call(
        second_kernel, "second", (*numbers, ylow, yacc, yloss, xloss, xgrad, *r3), (wide, thin, flat, wide, wide),
        out_specs=(VMEM, VMEM, VMEM, ANY, ANY), scratch_shapes=[pltpu.SemaphoreType.DMA],
    )
    image_grad, text_grad, loss = call(
        last_kernel, "last",
        (*numbers, image, text, ylow, yinv, yacc, loss, mean, r2_across, r2, image_grad, text_grad),
        (wide, wide, flat),
        in_specs=[VMEM] * 11 + [ANY] * 2, out_specs=(ANY, ANY, VMEM), input_output_aliases={11: 0, 12: 1},
        scratch_shapes=[
            pltpu.VMEM((rows, width), F32), pltpu.SemaphoreType.DMA((rows // TILE,)), pltpu.VMEM((rows, width), BF16),
        ],
    )
    return loss, image_grad, text_grad


def solution(mesh):
    in_specs = (P(AXES, None), P(AXES, None), P(), P())
    out_specs = (P(AXES), P(AXES, None), P(AXES, None))
    return jax.shard_map(body, mesh=mesh, in_specs=in_specs, out_specs=out_specs, check_vma=False)
```
